256 devices in a mesh: dp: 4 (over x_lo, core), blk: 64 (over z, y, x_hi).
Axes of the slice: x: 4 (x_hi: 2, x_lo: 2; x = x_hi * 2 + x_lo), y: 4, z: 8, core: 2. Of those that a mesh axis runs over, the one named last changes fastest.
Arguments:
- visual_features: bfloat16 [163840, 1152], P(('dp', 'blk')), parts along dimension 0, may hold values from -6 to 6
- caption_features: bfloat16 [163840, 1152], P(('dp', 'blk')), parts along dimension 0, may hold values from -6 to 6
- sharpness_scale: float32 [1], replicated, may hold values from 20 to 60
- score_shift: float32 [1], replicated, may hold values from -4 to -1
Outputs:
- image_grad: float32 [163840, 1152], P(('dp', 'blk')), parts along dimension 0
- text_grad: float32 [163840, 1152], P(('dp', 'blk')), parts along dimension 0
The draws below stay inside these ranges and needn't reach their ends.
There are 4 independent parts, one for each index of `dp`. The reference program is written for one: setup_inputs(seed, part) draws one part's arguments, and reference() takes and returns one part's arrays. A program takes and returns all parts, laid end to end along the dimension named above; an argument that names none is the same for every part. Nothing has to cross between parts.
All inputs are finite; a program needn't handle non-finite values.
Results may differ from the reference program's by a relative error of at most 0.0065.
Values may be sent and summed in bfloat16 or wider, within the bound.
No kernel may reach another device: no remote copies, remote signals or barrier semaphores. Data moves between devices by JAX's collectives and lax.ppermute only.
A program may use at most 64 MiB of HBM per device.

```python
import jax
import jax.numpy as jnp
from jax import lax

D = 1152
PAIRS_DEV = 640
STEPS = 4
PAIRS = 40960
N_BLK = 64


def levels(own_key, shape, cuts, least, high):
    def one(axis_at, shards_of):
        draws = jax.random.uniform(jax.random.fold_in(jax.random.fold_in(own_key, 6), axis_at), (shards_of,), jnp.float32, least / len(cuts), high / len(cuts))
        return jnp.repeat(jnp.exp(draws), shape[axis_at] // shards_of).reshape((-1,) + (1,) * (len(shape) - axis_at - 1))

    loudness = one(*cuts[0])
    for cut in cuts[1:]:
        loudness = loudness * one(*cut)
    return loudness


def bell_draw(stream_key, shape, deviation, most, cuts=(), kind=jnp.bfloat16):
    entries = jax.random.normal(stream_key, shape, jnp.float32) * deviation
    if len(cuts) > 0:
        entries = levels(stream_key, shape, cuts, -0.22, 0.18) * entries
    return jnp.clip(entries, min=-most, max=most).astype(kind)


def setup_inputs(seed: int = 0, part: int = 0) -> dict:
    keys = jax.random.split(jax.random.key(seed), 5)
    part_splits = jax.random.split(jax.random.fold_in(keys[4], part), 5)
    visual_features = bell_draw(part_splits[0], (PAIRS, D), 1.0, 6.0, ((0, 64),))
    caption_features = bell_draw(part_splits[1], (PAIRS, D), 1.0, 6.0, ((0, 64),))
    sharpness_scale = jnp.clip(jax.random.uniform(keys[2], (1,), jnp.float32, 20.0, 60.0), 20.0, 60.0)
    score_shift = jnp.clip(jax.random.uniform(keys[3], (1,), jnp.float32, -4.0, -1.0), -4.0, -1.0)
    return {"visual_features": visual_features, "caption_features": caption_features, "sharpness_scale": sharpness_scale, "score_shift": score_shift}


epsilon = 1e-06

def normalize(embedding_vector):
    values = embedding_vector.astype(jnp.float32)
    norms = jnp.sqrt(lax.optimization_barrier(jnp.sum(values * values, axis=1, keepdims=True)) + epsilon)
    return (values / norms, norms)

def pair_slopes(picture_block, text_block, score_factor, logit_bias, diagonal_mask):
    logits = score_factor * lax.dot_general(picture_block, text_block, (((1,), (1,)), ((), ())), preferred_element_type=jnp.float32) + logit_bias
    labels = jnp.float32(-1.0) + diagonal_mask * 2.0 * jnp.eye(picture_block.shape[0], dtype=jnp.float32)
    return (-labels * jax.nn.sigmoid(-labels * logits)).astype(jnp.bfloat16)

def project(gradient, units, norms):
    return (gradient - units * lax.optimization_barrier(jnp.sum(units * gradient, axis=1, keepdims=True))) / norms

def reference(visual_features, caption_features, sharpness_scale, score_shift):
    picture_unit_rows, image_norm = normalize(visual_features)
    caption_normalized, text_norm = normalize(caption_features)
    visual_portion = picture_unit_rows.astype(jnp.bfloat16)
    caption_portion = caption_normalized.astype(jnp.bfloat16)
    score_factor = sharpness_scale[0]
    logit_bias = score_shift[0]
    image_blocks = visual_portion.reshape(N_BLK, PAIRS_DEV, D)
    text_blocks = caption_portion.reshape(N_BLK, PAIRS_DEV, D)

    def per_block(totals, block):
        picture_block = image_blocks[block]
        image_part = jnp.zeros((PAIRS_DEV, D), jnp.float32)
        for offset in range(STEPS):
            target = ((block - offset) % N_BLK).astype(jnp.int32)
            visitor = text_blocks[target]
            pairwise_gradient = pair_slopes(picture_block, visitor, score_factor, logit_bias, jnp.float32(1.0 if offset == 0 else 0.0))
            image_part = image_part + score_factor * jnp.dot(pairwise_gradient, visitor, preferred_element_type=jnp.float32)
            contrib = score_factor * lax.dot_general(pairwise_gradient, picture_block, (((0,), (0,)), ((), ())), preferred_element_type=jnp.float32)
            totals = totals.at[target].add(contrib)
        return (totals, image_part)
    text_sums, image_sums = lax.scan(per_block, jnp.zeros((N_BLK, PAIRS_DEV, D), jnp.float32), jnp.arange(N_BLK, dtype=jnp.int32))
    image_grad = project(image_sums.reshape(PAIRS, D), picture_unit_rows, image_norm)
    text_grad = project(text_sums.reshape(PAIRS, D), caption_normalized, text_norm)
    return (image_grad, text_grad)
```

```python
import functools

import jax
import jax.numpy as jnp
from jax import lax
from jax.experimental import pallas as pl
from jax.experimental.pallas import tpu as pltpu
from jax.sharding import PartitionSpec as P

EPSILON = 1e-06
LOG2_E = 1.4426950408889634
FIRST = (256, 256, 128)
SECOND = (256, 256, 128)
PLAN = (
    ("go", "r10", "s20", "r11", "s10", "s21"),
    ("first",),
    ("wait", "r10", "s20"),
    ("go", "r20", "s22"),
    ("wait", "r11", "s21"),
    ("go", "r21", "q10"),
    ("wait", "s10", "s22"),
    ("go", "q11"),
    ("add", "s20", "s21", "s22", "r10", "r11", "s10"),
    ("wait", "r20"),
    ("go", "q20", "r12"),
    ("add", "q10", "r20"),
    ("wait", "r21"),
    ("go", "q21", "r22"),
    ("wait", "r12"),
    ("go", "q12"),
    ("add", "q11", "r12", "r21", "q20"),
    ("wait", "r22"),
    ("go", "q22"),
    ("end1", "q12", "r22", "q21"),
    ("last", "q22"),
)
TILE = 320


def normalized(rows):
    values = rows.astype(jnp.float32)
    norms = jnp.sqrt(jnp.sum(values * values, axis=1, keepdims=True) + EPSILON)
    return values / norms, norms


def against(scalars, own, partners, first_row=None):
    products = lax.dot_general(
        own, partners, (((1,), (1,)), ((), ())), preferred_element_type=jnp.float32
    )
    exponents = products * (-LOG2_E * scalars[0]) - LOG2_E * scalars[1]
    if first_row is not None:
        rows = lax.broadcasted_iota(jnp.int32, products.shape, 0) + first_row
        same = rows == lax.broadcasted_iota(jnp.int32, products.shape, 1)
        exponents = jnp.where(same, -exponents, exponents)
    slopes = 1.0 / (1.0 + jnp.exp2(exponents))
    if first_row is not None:
        slopes = jnp.where(same, -slopes, slopes)
    return jnp.dot(slopes.astype(jnp.bfloat16), partners, preferred_element_type=jnp.float32)


def tiles(rows):
    return [pl.ds(a, TILE) for a in range(0, rows, TILE)]


def fill(units, partners):
    at = 0
    for partner in partners:
        for a in range(0, partner.shape[0], 128):
            n = min(128, partner.shape[0] - a)
            units[at + a : at + a + n, :] = normalized(partner[a : a + n, :])[0].astype(
                jnp.bfloat16
            )
        at += partner.shape[0]


def first_kernel(scalars, own1, own2, unit1, unit2, sums1, sums2):
    fill(unit1, [own1])
    fill(unit2, [own2])
    for mine, other, sums in ((unit1, unit2, sums1), (unit2, unit1, sums2)):
        for a in range(0, mine.shape[0], TILE):
            sums[a : a + TILE, :] = against(scalars, mine[a : a + TILE, :], other[...], a)


def middle_kernel(n1, n2, scalars, unit1, unit2, old1, old2, *refs):
    partners1, partners2 = refs[:n1], refs[n1 : n1 + n2]
    sums1, sums2, scratch1, scratch2 = refs[n1 + n2 :]
    fill(scratch1, partners1)
    fill(scratch2, partners2)
    for mine, other, old, new in (
        (unit1, scratch1, old1, sums1),
        (unit2, scratch2, old2, sums2),
    ):
        for rows in tiles(mine.shape[0]):
            new[rows, :] = old[rows, :] + against(scalars, mine[rows, :], other[...])


def project(scalars, own, sums, first, outs, semaphores):
    rows = own.shape[0]
    step = 128
    for a in range(0, rows, step):
        piece = pl.ds(a, step)
        units, norms = normalized(own[piece, :])
        gradient = scalars[0] * sums[piece, :]
        along = jnp.sum(units * gradient, axis=1, keepdims=True)
        sums[piece, :] = (gradient - units * along) / norms

        def copy(which):
            return pltpu.make_async_copy(
                sums.at[piece, :], outs[which].at[piece, :], semaphores.at[a // step]
            )

        @pl.when(first)
        def _():
            copy(0).start()

        @pl.when(jnp.logical_not(first))
        def _():
            copy(1).start()

    for a in range(0, rows, step):
        piece = pl.ds(a, step)
        pltpu.make_async_copy(
            sums.at[piece, :], outs[0].at[piece, :], semaphores.at[a // step]
        ).wait()


def nearly_kernel(n1, n2, scalars, own1, unit1, unit2, old1, old2, *refs):
    partners1, partners2 = refs[:n1], refs[n1 : n1 + n2]
    out0, out1, sums2, scratch1, scratch2, total, semaphores = refs[n1 + n2 :]
    fill(scratch1, partners1)
    fill(scratch2, partners2)
    for rows in tiles(unit1.shape[0]):
        total[rows, :] = old1[rows, :] + against(scalars, unit1[rows, :], scratch1[...])
    for rows in tiles(unit2.shape[0]):
        sums2[rows, :] = old2[rows, :] + against(scalars, unit2[rows, :], scratch2[...])
    project(scalars, own1, total, scalars[2] > 0.5, (out0, out1), semaphores)


def last_kernel(n, scalars, own2, unit2, old2, *refs):
    out0, out1, scratch, total, semaphores = refs[n + 2 :]
    fill(scratch, refs[:n])
    for rows in tiles(unit2.shape[0]):
        total[rows, :] = old2[rows, :] + against(scalars, unit2[rows, :], scratch[...])
    project(scalars, own2, total, scalars[2] < 0.5, (out0, out1), semaphores)


VMEM = pl.BlockSpec(memory_space=pltpu.VMEM)
SMEM = pl.BlockSpec(memory_space=pltpu.SMEM)
HBM = pl.BlockSpec(memory_space=pl.ANY)


def call(kernel, operands, specs, out_shape, out_specs, scratch, pairs, aliases=None):
    width = operands[1].shape[1]
    return pl.pallas_call(
        kernel,
        in_specs=specs,
        out_specs=out_specs,
        out_shape=out_shape,
        scratch_shapes=scratch,
        input_output_aliases=aliases or {},
        cost_estimate=pl.CostEstimate(
            flops=4 * pairs * width, bytes_accessed=1 << 20, transcendentals=2 * pairs
        ),
        compiler_params=pltpu.CompilerParams(vmem_limit_bytes=20 * 1024 * 1024),
    )(*operands)


def shards(visual, caption, sharpness_scale, score_shift):
    blocks = lax.axis_size("blk")
    cells = blocks // 2
    even = lax.axis_index("blk") % 2 == 0
    rows, width = visual.shape

    def at(cell, half):
        return 2 * (cell % cells) + half

    cross = [(b, b ^ 1) for b in range(blocks)]
    outward = [(at(c, h), at(c + 1 - 2 * h, h)) for c in range(cells) for h in (0, 1)]
    inward = [(at(c, h), at(c - 1 + 2 * h, h)) for c in range(cells) for h in (0, 1)]

    def one(a, b):
        return jnp.where(even, caption[a:b], visual[a:b])

    def two(a, b):
        return jnp.where(even, visual[a:b], caption[a:b])

    def spans(sizes):
        ends = [sum(sizes[:k]) for k in range(len(sizes) + 1)]
        return list(zip(ends, ends[1:]))

    own1, own2 = one(0, rows), two(0, rows)
    flag = jnp.where(even, 0.0, 1.0)
    scalars = jnp.stack([sharpness_scale[0], score_shift[0], flag])

    real = jax.ShapeDtypeStruct((rows, width), jnp.float32)
    half = jax.ShapeDtypeStruct((rows, width), jnp.bfloat16)

    def count(partners):
        return sum(p.shape[0] for p in partners)

    def units_of(partners):
        return pltpu.VMEM((max(count(partners), 16), width), jnp.bfloat16)

    def middle(sums1, sums2, partners1, partners2):
        operands = [scalars, unit1, unit2, sums1, sums2, *partners1, *partners2]
        return call(
            functools.partial(middle_kernel, len(partners1), len(partners2)),
            operands,
            [SMEM] + [VMEM] * (len(operands) - 1),
            (real, real),
            (VMEM, VMEM),
            [units_of(partners1), units_of(partners2)],
            rows * count(partners1 + partners2),
            {3: 0, 4: 1},
        )

    def nearly(sums1, sums2, partners1, partners2):
        operands = [scalars, own1, unit1, unit2, sums1, sums2, *partners1, *partners2]
        return call(
            functools.partial(nearly_kernel, len(partners1), len(partners2)),
            operands,
            [SMEM] + [VMEM] * (len(operands) - 1),
            (real, real, real),
            (HBM, HBM, VMEM),
            [units_of(partners1), units_of(partners2), *staging],
            rows * count(partners1 + partners2),
            {5: 2},
        )

    def last(sums2, partners, out0, out1):
        operands = [scalars, own2, unit2, sums2, *partners, out0, out1]
        n = len(operands)
        return call(
            functools.partial(last_kernel, len(partners)),
            operands,
            [SMEM] + [VMEM] * (n - 3) + [HBM] * 2,
            (real, real),
            (HBM, HBM),
            [units_of(partners), *staging],
            rows * count(partners),
            {n - 2: 0, n - 1: 1},
        )

    staging = [
        pltpu.VMEM((rows, width), jnp.float32),
        pltpu.SemaphoreType.DMA((rows // 128,)),
    ]

    there, ready = {}, {}
    for k, (a, b) in enumerate(spans(FIRST)):
        ready["r1", k] = functools.partial(one, a, b)
        ready["q1", k] = functools.partial(there.get, ("r1", k))
    for k, (a, b) in enumerate(spans(SECOND)):
        ready["s2", k] = functools.partial(two, a, b)
        ready["r2", k] = functools.partial(there.get, ("s2", k))
        ready["q2", k] = functools.partial(there.get, ("r2", k))
    ready["s1", 0] = lambda: own1
    routes = {"r1": cross, "q1": inward, "s1": outward, "s2": inward, "r2": cross, "q2": outward}

    done = ()
    for action, *names in PLAN:
        names = [(n[:2], int(n[2:] or 0)) for n in names]
        if action == "wait":
            done = tuple(there[n] for n in names)
        elif action == "go":
            values = tuple(ready[n]() for n in names)
            if done:
                values = lax.optimization_barrier((values, done))[0]
            for n, value in zip(names, values):
                there[n] = lax.ppermute(value, "blk", routes[n[0]])
        elif action == "first":
            unit1, unit2, sums1, sums2 = call(
                first_kernel,
                [scalars, own1, own2],
                [SMEM, VMEM, VMEM],
                (half, half, real, real),
                (VMEM,) * 4,
                [],
                2 * rows * rows,
            )
        else:
            sides = [n for n in names if n[0] in ("s2", "r1", "q1")]
            ones, twos = [[there[n] for n in names if (n in sides) == s] for s in (True, False)]
            if action == "add":
                sums1, sums2 = middle(sums1, sums2, ones, twos)
            elif action == "end1":
                out0, out1, sums2 = nearly(sums1, sums2, ones, twos)
            else:
                return last(sums2, twos, out0, out1)


def solution(mesh):
    placed = (P(("dp", "blk"), None), P(("dp", "blk"), None), P(), P())
    return jax.shard_map(
        shards,
        mesh=mesh,
        in_specs=placed,
        out_specs=(P(("dp", "blk"), None), P(("dp", "blk"), None)),
        check_vma=False,
    )
```

```python
import functools

import jax
import jax.numpy as jnp
from jax import lax
from jax.experimental import pallas as pl
from jax.experimental.pallas import tpu as pltpu
from jax.sharding import PartitionSpec as P

EPSILON = 1e-06
LOG2_E = 1.4426950408889634
FIRST = (256, 256, 128)
SECOND = (256, 256, 128)
PLAN = (
    ("go", "r10", "s20", "r11", "s10", "s21"),
    ("first",),
    ("wait", "r10", "s20", "k1"),
    ("go", "r20", "s22"),
    ("wait", "r11", "s21"),
    ("go", "r21", "q10"),
    ("wait", "s10", "s22"),
    ("go", "q11"),
    ("add1", "s20", "s21", "s22", "r10", "r11"),
    ("add2", "s10"),
    ("wait", "r20", "k1", "k2"),
    ("go", "q20", "r12"),
    ("add1", "q10"),
    ("add2", "r20"),
    ("wait", "r21", "k1", "k2"),
    ("go", "q21", "r22"),
    ("wait", "r12"),
    ("go", "q12"),
    ("add1", "q11", "r12"),
    ("add2", "r21", "q20"),
    ("wait", "r22", "k1", "k2"),
    ("go", "q22"),
    ("end1", "q12"),
    ("add2", "r22", "q21"),
    ("end2", "q22"),
)
TILE = 320


def normalized(rows):
    values = rows.astype(jnp.float32)
    inverse = 1.0 / jnp.sqrt(jnp.sum(values * values, axis=1, keepdims=True) + EPSILON)
    return values * inverse, inverse


def slopes_of(scalars, own, partners, first_row=None):
    products = lax.dot_general(
        own, partners, (((1,), (1,)), ((), ())), preferred_element_type=jnp.float32
    )
    exponents = products * (-LOG2_E * scalars[0]) - LOG2_E * scalars[1]
    if first_row is not None:
        rows = lax.broadcasted_iota(jnp.int32, products.shape, 0) + first_row
        same = rows == lax.broadcasted_iota(jnp.int32, products.shape, 1)
        exponents = jnp.where(same, -exponents, exponents)
    slopes = 1.0 / (1.0 + jnp.exp2(exponents))
    if first_row is not None:
        slopes = jnp.where(same, -slopes, slopes)
    return slopes.astype(jnp.bfloat16)


def against(scalars, own, partners):
    return jnp.dot(
        slopes_of(scalars, own, partners), partners, preferred_element_type=jnp.float32
    )


def tiles(rows):
    return [pl.ds(a, TILE) for a in range(0, rows, TILE)]


def fill(units, partners):
    at = 0
    for partner in partners:
        for a in range(0, partner.shape[0], 128):
            n = min(128, partner.shape[0] - a)
            units[at + a : at + a + n, :] = normalized(partner[a : a + n, :])[0].astype(
                jnp.bfloat16
            )
        at += partner.shape[0]


def first_kernel(scalars, own1, own2, unit1, unit2, sums1, sums2, slopes):
    fill(unit1, [own1])
    fill(unit2, [own2])
    for a in range(0, own1.shape[0], TILE):
        rows = pl.ds(a, TILE)
        slopes[rows, :] = slopes_of(scalars, unit1[rows, :], unit2[...], a)
        sums1[rows, :] = jnp.dot(
            slopes[rows, :], unit2[...], preferred_element_type=jnp.float32
        )
    sums2[...] = lax.dot_general(
        slopes[...], unit1[...], (((0,), (0,)), ((), ())), preferred_element_type=jnp.float32
    )


def middle_kernel(n, scalars, unit, old, *refs):
    sums, scratch = refs[n:]
    fill(scratch, refs[:n])
    for rows in tiles(unit.shape[0]):
        sums[rows, :] = old[rows, :] + against(scalars, unit[rows, :], scratch[...])


def project(scalars, own, sums, first, outs, semaphores):
    rows = own.shape[0]
    step = 128
    for a in range(0, rows, step):
        piece = pl.ds(a, step)
        units, inverse = normalized(own[piece, :])
        gradient = scalars[0] * sums[piece, :]
        along = jnp.sum(units * gradient, axis=1, keepdims=True)
        sums[piece, :] = (gradient - units * along) * inverse

        def copy(which):
            return pltpu.make_async_copy(
                sums.at[piece, :], outs[which].at[piece, :], semaphores.at[a // step]
            )

        @pl.when(first)
        def _():
            copy(0).start()

        @pl.when(jnp.logical_not(first))
        def _():
            copy(1).start()

    for a in range(0, rows, step):
        piece = pl.ds(a, step)
        pltpu.make_async_copy(
            sums.at[piece, :], outs[0].at[piece, :], semaphores.at[a // step]
        ).wait()


def last_kernel(n, side, scalars, own, unit, old, *refs):
    out0, out1, scratch, total, semaphores = refs[-5:]
    fill(scratch, refs[:n])
    for rows in tiles(unit.shape[0]):
        total[rows, :] = old[rows, :] + against(scalars, unit[rows, :], scratch[...])
    first = scalars[2] > 0.5 if side == 1 else scalars[2] < 0.5
    project(scalars, own, total, first, (out0, out1), semaphores)


VMEM = pl.BlockSpec(memory_space=pltpu.VMEM)
SMEM = pl.BlockSpec(memory_space=pltpu.SMEM)
HBM = pl.BlockSpec(memory_space=pl.ANY)


def call(kernel, operands, specs, out_shape, out_specs, scratch, pairs, aliases=None):
    width = operands[1].shape[1]
    return pl.pallas_call(
        kernel,
        in_specs=specs,
        out_specs=out_specs,
        out_shape=out_shape,
        scratch_shapes=scratch,
        input_output_aliases=aliases or {},
        cost_estimate=pl.CostEstimate(
            flops=4 * pairs * width, bytes_accessed=1 << 20, transcendentals=2 * pairs
        ),
        compiler_params=pltpu.CompilerParams(vmem_limit_bytes=20 * 1024 * 1024),
    )(*operands)


def shards(visual, caption, sharpness_scale, score_shift):
    blocks = lax.axis_size("blk")
    cells = blocks // 2
    even = lax.axis_index("blk") % 2 == 0
    rows, width = visual.shape

    def at(cell, half):
        return 2 * (cell % cells) + half

    cross = [(b, b ^ 1) for b in range(blocks)]
    outward = [(at(c, h), at(c + 1 - 2 * h, h)) for c in range(cells) for h in (0, 1)]
    inward = [(at(c, h), at(c - 1 + 2 * h, h)) for c in range(cells) for h in (0, 1)]

    def one(a, b):
        return jnp.where(even, caption[a:b], visual[a:b])

    def two(a, b):
        return jnp.where(even, visual[a:b], caption[a:b])

    def spans(sizes):
        ends = [sum(sizes[:k]) for k in range(len(sizes) + 1)]
        return list(zip(ends, ends[1:]))

    own1, own2 = one(0, rows), two(0, rows)
    flag = jnp.where(even, 0.0, 1.0)
    scalars = jnp.stack([sharpness_scale[0], score_shift[0], flag])

    real = jax.ShapeDtypeStruct((rows, width), jnp.float32)
    half = jax.ShapeDtypeStruct((rows, width), jnp.bfloat16)

    def count(partners):
        return sum(p.shape[0] for p in partners)

    def units_of(partners):
        return pltpu.VMEM((max(count(partners), 16), width), jnp.bfloat16)

    def middle(unit, sums, partners):
        operands = [scalars, unit, sums, *partners]
        return call(
            functools.partial(middle_kernel, len(partners)),
            operands,
            [SMEM] + [VMEM] * (len(operands) - 1),
            real,
            VMEM,
            [units_of(partners)],
            rows * count(partners),
            {2: 0},
        )

    def last(side, own, unit, sums, partners, outs):
        operands = [scalars, own, unit, sums, *partners, *outs]
        n = len(operands)
        return call(
            functools.partial(last_kernel, len(partners), side),
            operands,
            [SMEM] + [VMEM] * (n - 1 - len(outs)) + [HBM] * len(outs),
            (real, real),
            (HBM, HBM),
            [units_of(partners), *staging],
            rows * count(partners),
            {n - 2: 0, n - 1: 1} if outs else {},
        )

    staging = [
        pltpu.VMEM((rows, width), jnp.float32),
        pltpu.SemaphoreType.DMA((rows // 128,)),
    ]

    there, ready = {}, {}
    for k, (a, b) in enumerate(spans(FIRST)):
        ready["r1", k] = functools.partial(one, a, b)
        ready["q1", k] = functools.partial(there.get, ("r1", k))
    for k, (a, b) in enumerate(spans(SECOND)):
        ready["s2", k] = functools.partial(two, a, b)
        ready["r2", k] = functools.partial(there.get, ("s2", k))
        ready["q2", k] = functools.partial(there.get, ("r2", k))
    ready["s1", 0] = lambda: own1
    routes = {"r1": cross, "q1": inward, "s1": outward, "s2": inward, "r2": cross, "q2": outward}

    done, outs = (), ()
    sums, units = {}, {}
    for action, *names in PLAN:
        names = [(n[:2], int(n[2:] or 0)) for n in names]
        if action == "wait":
            done = tuple(there[n] if n in there else sums[int(n[0][1])] for n in names)
        elif action == "go":
            values = tuple(ready[n]() for n in names)
            if done:
                values = lax.optimization_barrier((values, done))[0]
            for n, value in zip(names, values):
                there[n] = lax.ppermute(value, "blk", routes[n[0]])
        elif action == "first":
            units[1], units[2], sums[1], sums[2] = call(
                first_kernel,
                [scalars, own1, own2],
                [SMEM, VMEM, VMEM],
                (half, half, real, real),
                (VMEM,) * 4,
                [pltpu.VMEM((rows, rows), jnp.bfloat16)],
                2 * rows * rows,
            )
        else:
            side = int(action[-1])
            partners = [there[n] for n in names]
            if action[:-1] == "add":
                sums[side] = middle(units[side], sums[side], partners)
            else:
                outs = last(side, (own1, own2)[side - 1], units[side], sums[side], partners, outs)
    return outs


def solution(mesh):
    placed = (P(("dp", "blk"), None), P(("dp", "blk"), None), P(), P())
    return jax.shard_map(
        shards,
        mesh=mesh,
        in_specs=placed,
        out_specs=(P(("dp", "blk"), None), P(("dp", "blk"), None)),
        check_vma=False,
    )
```

```python
import functools

import jax
import jax.numpy as jnp
from jax import lax
from jax.experimental import pallas as pl
from jax.experimental.pallas import tpu as pltpu
from jax.sharding import PartitionSpec as P

EPSILON = 1e-06
LOG2_E = 1.4426950408889634
FIRST = (256, 256, 128)
SECOND = (256, 256, 128)
PLAN = (
    ("go", "r10", "s20", "r11", "s10", "s21"),
    ("first",),
    ("wait", "r10", "s20", "k1"),
    ("go", "r20", "s22"),
    ("wait", "r11", "s21"),
    ("go", "r21", "q10"),
    ("wait", "s10", "s22"),
    ("go", "q11"),
    ("add1", "s20", "s21", "s22", "r10", "r11"),
    ("wait", "r20", "k1"),
    ("go", "q20", "r12"),
    ("add2", "s10", "r20"),
    ("wait", "r21", "q10", "k2"),
    ("go", "q21", "r22"),
    ("add2", "r21", "q20"),
    ("wait", "r12", "k2"),
    ("go", "q12"),
    ("add1", "q10", "q11", "r12"),
    ("wait", "r22", "k1"),
    ("go", "q22"),
    ("end1", "q12"),
    ("add2", "r22", "q21"),
    ("end2", "q22"),
)
TILE = 320


def normalized(rows):
    values = rows.astype(jnp.float32)
    inverse = 1.0 / jnp.sqrt(jnp.sum(values * values, axis=1, keepdims=True) + EPSILON)
    return values * inverse, inverse


def slopes_of(scalars, own, partners, first_row=None):
    products = lax.dot_general(
        own, partners, (((1,), (1,)), ((), ())), preferred_element_type=jnp.float32
    )
    exponents = products * (-LOG2_E * scalars[0]) - LOG2_E * scalars[1]
    if first_row is not None:
        rows = lax.broadcasted_iota(jnp.int32, products.shape, 0) + first_row
        same = rows == lax.broadcasted_iota(jnp.int32, products.shape, 1)
        exponents = jnp.where(same, -exponents, exponents)
    slopes = 1.0 / (1.0 + jnp.exp2(exponents))
    if first_row is not None:
        slopes = jnp.where(same, -slopes, slopes)
    return slopes.astype(jnp.bfloat16)


def against(scalars, own, partners):
    return jnp.dot(
        slopes_of(scalars, own, partners), partners, preferred_element_type=jnp.float32
    )


def tiles(rows):
    return [pl.ds(a, TILE) for a in range(0, rows, TILE)]


def fill(units, partners):
    at = 0
    for partner in partners:
        for a in range(0, partner.shape[0], 128):
            n = min(128, partner.shape[0] - a)
            units[at + a : at + a + n, :] = normalized(partner[a : a + n, :])[0].astype(
                jnp.bfloat16
            )
        at += partner.shape[0]


def first_kernel(scalars, own1, own2, unit1, unit2, sums1, sums2, slopes):
    fill(unit1, [own1])
    fill(unit2, [own2])
    for a in range(0, own1.shape[0], TILE):
        rows = pl.ds(a, TILE)
        slopes[rows, :] = slopes_of(scalars, unit1[rows, :], unit2[...], a)
        sums1[rows, :] = jnp.dot(
            slopes[rows, :], unit2[...], preferred_element_type=jnp.float32
        )
    sums2[...] = lax.dot_general(
        slopes[...], unit1[...], (((0,), (0,)), ((), ())), preferred_element_type=jnp.float32
    )


def middle_kernel(n, scalars, unit, old, *refs):
    sums, scratch = refs[n:]
    fill(scratch, refs[:n])
    for rows in tiles(unit.shape[0]):
        sums[rows, :] = old[rows, :] + against(scalars, unit[rows, :], scratch[...])


def project(scalars, own, sums, first, outs, semaphores):
    rows = own.shape[0]
    step = 128
    for a in range(0, rows, step):
        piece = pl.ds(a, step)
        units, inverse = normalized(own[piece, :])
        gradient = scalars[0] * sums[piece, :]
        along = jnp.sum(units * gradient, axis=1, keepdims=True)
        sums[piece, :] = (gradient - units * along) * inverse

        def copy(which):
            return pltpu.make_async_copy(
                sums.at[piece, :], outs[which].at[piece, :], semaphores.at[a // step]
            )

        @pl.when(first)
        def _():
            copy(0).start()

        @pl.when(jnp.logical_not(first))
        def _():
            copy(1).start()

    for a in range(0, rows, step):
        piece = pl.ds(a, step)
        pltpu.make_async_copy(
            sums.at[piece, :], outs[0].at[piece, :], semaphores.at[a // step]
        ).wait()


def last_kernel(n, side, scalars, own, unit, old, *refs):
    out0, out1, scratch, total, semaphores = refs[-5:]
    fill(scratch, refs[:n])
    for rows in tiles(unit.shape[0]):
        total[rows, :] = old[rows, :] + against(scalars, unit[rows, :], scratch[...])
    first = scalars[2] > 0.5 if side == 1 else scalars[2] < 0.5
    project(scalars, own, total, first, (out0, out1), semaphores)


VMEM = pl.BlockSpec(memory_space=pltpu.VMEM)
SMEM = pl.BlockSpec(memory_space=pltpu.SMEM)
HBM = pl.BlockSpec(memory_space=pl.ANY)


def call(kernel, operands, specs, out_shape, out_specs, scratch, pairs, aliases=None):
    width = operands[1].shape[1]
    return pl.pallas_call(
        kernel,
        in_specs=specs,
        out_specs=out_specs,
        out_shape=out_shape,
        scratch_shapes=scratch,
        input_output_aliases=aliases or {},
        cost_estimate=pl.CostEstimate(
            flops=4 * pairs * width, bytes_accessed=1 << 20, transcendentals=2 * pairs
        ),
        compiler_params=pltpu.CompilerParams(vmem_limit_bytes=20 * 1024 * 1024),
    )(*operands)


def shards(visual, caption, sharpness_scale, score_shift):
    blocks = lax.axis_size("blk")
    cells = blocks // 2
    even = lax.axis_index("blk") % 2 == 0
    rows, width = visual.shape

    def at(cell, half):
        return 2 * (cell % cells) + half

    cross = [(b, b ^ 1) for b in range(blocks)]
    outward = [(at(c, h), at(c + 1 - 2 * h, h)) for c in range(cells) for h in (0, 1)]
    inward = [(at(c, h), at(c - 1 + 2 * h, h)) for c in range(cells) for h in (0, 1)]

    def one(a, b):
        return jnp.where(even, caption[a:b], visual[a:b])

    def two(a, b):
        return jnp.where(even, visual[a:b], caption[a:b])

    def spans(sizes):
        ends = [sum(sizes[:k]) for k in range(len(sizes) + 1)]
        return list(zip(ends, ends[1:]))

    heads = one(0, FIRST[0]), two(0, SECOND[0])
    caption, visual = lax.optimization_barrier((caption, visual, heads))[:2]
    own1, own2 = one(0, rows), two(0, rows)
    flag = jnp.where(even, 0.0, 1.0)
    scalars = jnp.stack([sharpness_scale[0], score_shift[0], flag])

    real = jax.ShapeDtypeStruct((rows, width), jnp.float32)
    half = jax.ShapeDtypeStruct((rows, width), jnp.bfloat16)

    def count(partners):
        return sum(p.shape[0] for p in partners)

    def units_of(partners):
        return pltpu.VMEM((max(count(partners), 16), width), jnp.bfloat16)

    def middle(unit, sums, partners):
        operands = [scalars, unit, sums, *partners]
        return call(
            functools.partial(middle_kernel, len(partners)),
            operands,
            [SMEM] + [VMEM] * (len(operands) - 1),
            real,
            VMEM,
            [units_of(partners)],
            rows * count(partners),
            {2: 0},
        )

    def last(side, own, unit, sums, partners, outs):
        operands = [scalars, own, unit, sums, *partners, *outs]
        n = len(operands)
        return call(
            functools.partial(last_kernel, len(partners), side),
            operands,
            [SMEM] + [VMEM] * (n - 1 - len(outs)) + [HBM] * len(outs),
            (real, real),
            (HBM, HBM),
            [units_of(partners), *staging],
            rows * count(partners),
            {n - 2: 0, n - 1: 1} if outs else {},
        )

    staging = [
        pltpu.VMEM((rows, width), jnp.float32),
        pltpu.SemaphoreType.DMA((rows // 128,)),
    ]

    there, ready = {}, {}
    for k, (a, b) in enumerate(spans(FIRST)):
        ready["r1", k] = functools.partial(one, a, b)
        ready["q1", k] = functools.partial(there.get, ("r1", k))
    for k, (a, b) in enumerate(spans(SECOND)):
        ready["s2", k] = functools.partial(two, a, b)
        ready["r2", k] = functools.partial(there.get, ("s2", k))
        ready["q2", k] = functools.partial(there.get, ("r2", k))
    ready["r1", 0], ready["s2", 0] = lambda: heads[0], lambda: heads[1]
    ready["s1", 0] = lambda: own1
    routes = {"r1": cross, "q1": inward, "s1": outward, "s2": inward, "r2": cross, "q2": outward}

    done, outs = (), ()
    sums, units = {}, {}
    for action, *names in PLAN:
        names = [(n[:2], int(n[2:] or 0)) for n in names]
        if action == "wait":
            done = tuple(there[n] if n in there else sums[int(n[0][1])] for n in names)
        elif action == "go":
            values = tuple(ready[n]() for n in names)
            if done:
                values = lax.optimization_barrier((values, done))[0]
            for n, value in zip(names, values):
                there[n] = lax.ppermute(value, "blk", routes[n[0]])
        elif action == "first":
            units[1], units[2], sums[1], sums[2] = call(
                first_kernel,
                [scalars, own1, own2],
                [SMEM, VMEM, VMEM],
                (half, half, real, real),
                (VMEM,) * 4,
                [pltpu.VMEM((rows, rows), jnp.bfloat16)],
                2 * rows * rows,
            )
        else:
            side = int(action[-1])
            partners = [there[n] for n in names]
            if action[:-1] == "add":
                sums[side] = middle(units[side], sums[side], partners)
            else:
                outs = last(side, (own1, own2)[side - 1], units[side], sums[side], partners, outs)
    return outs


def solution(mesh):
    placed = (P(("dp", "blk"), None), P(("dp", "blk"), None), P(), P())
    return jax.shard_map(
        shards,
        mesh=mesh,
        in_specs=placed,
        out_specs=(P(("dp", "blk"), None), P(("dp", "blk"), None)),
        check_vma=False,
    )
```

```python
import functools

import jax
import jax.numpy as jnp
from jax import lax
from jax.experimental import pallas as pl
from jax.experimental.pallas import tpu as pltpu
from jax.sharding import PartitionSpec as P

EPSILON = 1e-06
LOG2_E = 1.4426950408889634
FIRST = (256, 256, 128)
SECOND = (256, 256, 128)
PLAN = (
    ("go", "r10", "s20", "r11", "s10", "s21"),
    ("first",),
    ("wait", "r10", "s20", "k1"),
    ("go", "r20", "s22"),
    ("wait", "r11", "s21"),
    ("go", "r21", "q10"),
    ("wait", "s10", "s22"),
    ("go", "q11"),
    ("add1", "s20", "s21", "s22", "r10", "r11"),
    ("wait", "r20", "k1"),
    ("go", "q20", "r12"),
    ("add2", "s10", "r20"),
    ("wait", "r21", "q10", "k2"),
    ("go", "q21", "r22"),
    ("add2", "r21", "q20"),
    ("wait", "r12", "k2"),
    ("go", "q12"),
    ("add1", "q10", "q11", "r12"),
    ("wait", "r22", "k1"),
    ("go", "q22"),
    ("end1", "q12"),
    ("add2", "r22", "q21"),
    ("end2", "q22"),
)
TILE = 320


def normalized(rows):
    values = rows.astype(jnp.float32)
    inverse = 1.0 / jnp.sqrt(jnp.sum(values * values, axis=1, keepdims=True) + EPSILON)
    return values * inverse, inverse


def slopes_of(scalars, own, partners, first_row=None):
    products = lax.dot_general(
        own, partners, (((1,), (1,)), ((), ())), preferred_element_type=jnp.float32
    )
    exponents = products * (-LOG2_E * scalars[0:1, 0:1]) - LOG2_E * scalars[1:2, 0:1]
    if first_row is not None:
        rows = lax.broadcasted_iota(jnp.int32, products.shape, 0) + first_row
        same = rows == lax.broadcasted_iota(jnp.int32, products.shape, 1)
        exponents = jnp.where(same, -exponents, exponents)
    slopes = 1.0 / (1.0 + jnp.exp2(exponents))
    if first_row is not None:
        slopes = jnp.where(same, -slopes, slopes)
    return slopes.astype(jnp.bfloat16)


def against(scalars, own, partners):
    return jnp.dot(
        slopes_of(scalars, own, partners), partners, preferred_element_type=jnp.float32
    )


def tiles(rows):
    return [pl.ds(a, TILE) for a in range(0, rows, TILE)]


def fill(units, partners):
    at = 0
    for partner in partners:
        for a in range(0, partner.shape[0], 128):
            n = min(128, partner.shape[0] - a)
            units[at + a : at + a + n, :] = normalized(partner[a : a + n, :])[0].astype(
                jnp.bfloat16
            )
        at += partner.shape[0]


def first_kernel(scalars, own1, own2, unit1, unit2, sums1, sums2, slopes):
    fill(unit1, [own1])
    fill(unit2, [own2])
    for a in range(0, own1.shape[0], TILE):
        rows = pl.ds(a, TILE)
        slopes[rows, :] = slopes_of(scalars, unit1[rows, :], unit2[...], a)
        sums1[rows, :] = jnp.dot(
            slopes[rows, :], unit2[...], preferred_element_type=jnp.float32
        )
    sums2[...] = lax.dot_general(
        slopes[...], unit1[...], (((0,), (0,)), ((), ())), preferred_element_type=jnp.float32
    )


def middle_kernel(n, scalars, unit, old, *refs):
    sums, scratch = refs[n:]
    fill(scratch, refs[:n])
    for rows in tiles(unit.shape[0]):
        sums[rows, :] = old[rows, :] + against(scalars, unit[rows, :], scratch[...])


def project(scalars, own, sums, first, outs, semaphores):
    rows = own.shape[0]
    step = 128
    for a in range(0, rows, step):
        piece = pl.ds(a, step)
        units, inverse = normalized(own[piece, :])
        gradient = scalars[0:1, 0:1] * sums[piece, :]
        along = jnp.sum(units * gradient, axis=1, keepdims=True)
        sums[piece, :] = (gradient - units * along) * inverse

        def copy(which):
            return pltpu.make_async_copy(
                sums.at[piece, :], outs[which].at[piece, :], semaphores.at[a // step]
            )

        @pl.when(first)
        def _():
            copy(0).start()

        @pl.when(jnp.logical_not(first))
        def _():
            copy(1).start()

    for a in range(0, rows, step):
        piece = pl.ds(a, step)
        pltpu.make_async_copy(
            sums.at[piece, :], outs[0].at[piece, :], semaphores.at[a // step]
        ).wait()


def last_kernel(n, side, scalars, own, unit, old, *refs):
    out0, out1, scratch, total, semaphores = refs[-5:]
    fill(scratch, refs[:n])
    for rows in tiles(unit.shape[0]):
        total[rows, :] = old[rows, :] + against(scalars, unit[rows, :], scratch[...])
    first = jnp.max(scalars[2:3, :]) > 0.5 if side == 1 else jnp.max(scalars[2:3, :]) < 0.5
    project(scalars, own, total, first, (out0, out1), semaphores)


VMEM = pl.BlockSpec(memory_space=pltpu.VMEM)
HBM = pl.BlockSpec(memory_space=pl.ANY)


def call(kernel, operands, specs, out_shape, out_specs, scratch, pairs, aliases=None):
    width = operands[1].shape[1]
    return pl.pallas_call(
        kernel,
        in_specs=specs,
        out_specs=out_specs,
        out_shape=out_shape,
        scratch_shapes=scratch,
        input_output_aliases=aliases or {},
        cost_estimate=pl.CostEstimate(
            flops=4 * pairs * width, bytes_accessed=1 << 20, transcendentals=2 * pairs
        ),
        compiler_params=pltpu.CompilerParams(vmem_limit_bytes=20 * 1024 * 1024),
    )(*operands)


def shards(visual, caption, sharpness_scale, score_shift):
    blocks = lax.axis_size("blk")
    cells = blocks // 2
    even = lax.axis_index("blk") % 2 == 0
    rows, width = visual.shape

    def at(cell, half):
        return 2 * (cell % cells) + half

    cross = [(b, b ^ 1) for b in range(blocks)]
    outward = [(at(c, h), at(c + 1 - 2 * h, h)) for c in range(cells) for h in (0, 1)]
    inward = [(at(c, h), at(c - 1 + 2 * h, h)) for c in range(cells) for h in (0, 1)]

    def one(a, b):
        return jnp.where(even, caption[a:b], visual[a:b])

    def two(a, b):
        return jnp.where(even, visual[a:b], caption[a:b])

    def spans(sizes):
        ends = [sum(sizes[:k]) for k in range(len(sizes) + 1)]
        return list(zip(ends, ends[1:]))

    heads = one(0, FIRST[0]), two(0, SECOND[0])
    caption, visual = lax.optimization_barrier((caption, visual, heads))[:2]
    own1, own2 = one(0, rows), two(0, rows)
    flag = jnp.where(even, 0.0, 1.0)
    row = lax.broadcasted_iota(jnp.int32, (8, 128), 0)
    scalars = jnp.where(row == 0, sharpness_scale[0], jnp.where(row == 1, score_shift[0], flag))

    real = jax.ShapeDtypeStruct((rows, width), jnp.float32)
    half = jax.ShapeDtypeStruct((rows, width), jnp.bfloat16)

    def count(partners):
        return sum(p.shape[0] for p in partners)

    def units_of(partners):
        return pltpu.VMEM((max(count(partners), 16), width), jnp.bfloat16)

    def middle(unit, sums, partners):
        operands = [scalars, unit, sums, *partners]
        return call(
            functools.partial(middle_kernel, len(partners)),
            operands,
            [VMEM] + [VMEM] * (len(operands) - 1),
            real,
            VMEM,
            [units_of(partners)],
            rows * count(partners),
            {2: 0},
        )

    def last(side, own, unit, sums, partners, outs):
        operands = [scalars, own, unit, sums, *partners, *outs]
        n = len(operands)
        return call(
            functools.partial(last_kernel, len(partners), side),
            operands,
            [VMEM] + [VMEM] * (n - 1 - len(outs)) + [HBM] * len(outs),
            (real, real),
            (HBM, HBM),
            [units_of(partners), *staging],
            rows * count(partners),
            {n - 2: 0, n - 1: 1} if outs else {},
        )

    staging = [
        pltpu.VMEM((rows, width), jnp.float32),
        pltpu.SemaphoreType.DMA((rows // 128,)),
    ]

    there, ready = {}, {}
    for k, (a, b) in enumerate(spans(FIRST)):
        ready["r1", k] = functools.partial(one, a, b)
        ready["q1", k] = functools.partial(there.get, ("r1", k))
    for k, (a, b) in enumerate(spans(SECOND)):
        ready["s2", k] = functools.partial(two, a, b)
        ready["r2", k] = functools.partial(there.get, ("s2", k))
        ready["q2", k] = functools.partial(there.get, ("r2", k))
    ready["r1", 0], ready["s2", 0] = lambda: heads[0], lambda: heads[1]
    ready["s1", 0] = lambda: own1
    routes = {"r1": cross, "q1": inward, "s1": outward, "s2": inward, "r2": cross, "q2": outward}

    done, outs = (), ()
    sums, units = {}, {}
    for action, *names in PLAN:
        names = [(n[:2], int(n[2:] or 0)) for n in names]
        if action == "wait":
            done = tuple(there[n] if n in there else sums[int(n[0][1])] for n in names)
        elif action == "go":
            values = tuple(ready[n]() for n in names)
            if done:
                values = lax.optimization_barrier((values, done))[0]
            for n, value in zip(names, values):
                there[n] = lax.ppermute(value, "blk", routes[n[0]])
        elif action == "first":
            units[1], units[2], sums[1], sums[2] = call(
                first_kernel,
                [scalars, own1, own2],
                [VMEM, VMEM, VMEM],
                (half, half, real, real),
                (VMEM,) * 4,
                [pltpu.VMEM((rows, rows), jnp.bfloat16)],
                2 * rows * rows,
            )
        else:
            side = int(action[-1])
            partners = [there[n] for n in names]
            if action[:-1] == "add":
                sums[side] = middle(units[side], sums[side], partners)
            else:
                outs = last(side, (own1, own2)[side - 1], units[side], sums[side], partners, outs)
    return outs


def solution(mesh):
    placed = (P(("dp", "blk"), None), P(("dp", "blk"), None), P(), P())
    return jax.shard_map(
        shards,
        mesh=mesh,
        in_specs=placed,
        out_specs=(P(("dp", "blk"), None), P(("dp", "blk"), None)),
        check_vma=False,
    )
```

```python
import functools

import jax
import jax.numpy as jnp
from jax import lax
from jax.experimental import pallas as pl
from jax.experimental.pallas import tpu as pltpu
from jax.sharding import PartitionSpec as P

EPSILON = 1e-06
LOG2_E = 1.4426950408889634
FIRST = (256, 256, 128)
SECOND = (256, 256, 128)
PLAN = (
    ("go", "r10", "s20", "r11", "s10", "s21"),
    ("first",),
    ("wait", "r10", "s20", "k1"),
    ("go", "r20", "s22"),
    ("wait", "r11", "s21"),
    ("go", "r21", "q10"),
    ("wait", "s10", "s22"),
    ("go", "q11"),
    ("add1", "s20", "s21", "s22", "r10", "r11"),
    ("wait", "r20", "k1"),
    ("go", "q20", "r12"),
    ("add2", "s10", "r20"),
    ("wait", "r21", "q10", "k2"),
    ("go", "q21", "r22"),
    ("add2", "r21", "q20"),
    ("wait", "r12", "k2"),
    ("go", "q12"),
    ("add1", "q10", "q11", "r12"),
    ("wait", "r22", "k1"),
    ("go", "q22"),
    ("end1", "q12"),
    ("add2", "r22", "q21"),
    ("end2", "q22"),
)
TILE = 320


def normalized(rows):
    values = rows.astype(jnp.float32)
    inverse = 1.0 / jnp.sqrt(jnp.sum(values * values, axis=1, keepdims=True) + EPSILON)
    return values * inverse, inverse


def slopes_of(scalars, own, partners, first_row=None):
    products = lax.dot_general(
        own, partners, (((1,), (1,)), ((), ())), preferred_element_type=jnp.float32
    )
    exponents = products * (-LOG2_E * scalars[0:1, 0:1]) - LOG2_E * scalars[1:2, 0:1]
    if first_row is not None:
        rows = lax.broadcasted_iota(jnp.int32, products.shape, 0) + first_row
        same = rows == lax.broadcasted_iota(jnp.int32, products.shape, 1)
        exponents = jnp.where(same, -exponents, exponents)
    slopes = 1.0 / (1.0 + jnp.exp2(exponents))
    if first_row is not None:
        slopes = jnp.where(same, -slopes, slopes)
    return slopes.astype(jnp.bfloat16)


def against(scalars, own, partners):
    return jnp.dot(
        slopes_of(scalars, own, partners), partners, preferred_element_type=jnp.float32
    )


def tiles(rows):
    return [pl.ds(a, TILE) for a in range(0, rows, TILE)]


def fill(units, partners):
    at = 0
    for partner in partners:
        for a in range(0, partner.shape[0], 128):
            n = min(128, partner.shape[0] - a)
            units[at + a : at + a + n, :] = normalized(partner[a : a + n, :])[0].astype(
                jnp.bfloat16
            )
        at += partner.shape[0]


def first_kernel(scalars, own1, own2, unit1, unit2, sums1, sums2, slopes):
    fill(unit1, [own1])
    fill(unit2, [own2])
    for a in range(0, own1.shape[0], TILE):
        rows = pl.ds(a, TILE)
        slopes[rows, :] = slopes_of(scalars, unit1[rows, :], unit2[...], a)
        sums1[rows, :] = jnp.dot(
            slopes[rows, :], unit2[...], preferred_element_type=jnp.float32
        )
    sums2[...] = lax.dot_general(
        slopes[...], unit1[...], (((0,), (0,)), ((), ())), preferred_element_type=jnp.float32
    )


def middle_kernel(n, scalars, unit, old, *refs):
    sums, scratch = refs[n:]
    fill(scratch, refs[:n])
    for rows in tiles(unit.shape[0]):
        sums[rows, :] = old[rows, :] + against(scalars, unit[rows, :], scratch[...])


def project(scalars, own, sums, first, outs, semaphores, begin):
    step = TILE // 2
    for a in range(begin, begin + TILE, step):
        piece = pl.ds(a, step)
        units, inverse = normalized(own[piece, :])
        gradient = scalars[0:1, 0:1] * sums[piece, :]
        along = jnp.sum(units * gradient, axis=1, keepdims=True)
        sums[piece, :] = (gradient - units * along) * inverse

        def copy(which):
            return pltpu.make_async_copy(
                sums.at[piece, :], outs[which].at[piece, :], semaphores.at[a // step]
            )

        @pl.when(first)
        def _():
            copy(0).start()

        @pl.when(jnp.logical_not(first))
        def _():
            copy(1).start()


def last_kernel(n, side, scalars, own, unit, old, *refs):
    out0, out1, scratch, total, semaphores = refs[-5:]
    fill(scratch, refs[:n])
    flag = jnp.max(scalars[2:3, :])
    first = flag > 0.5 if side == 1 else flag < 0.5
    for a in range(0, unit.shape[0], TILE):
        rows = pl.ds(a, TILE)
        total[rows, :] = old[rows, :] + against(scalars, unit[rows, :], scratch[...])
        project(scalars, own, total, first, (out0, out1), semaphores, a)
    step = TILE // 2
    for a in range(0, unit.shape[0], step):
        piece = pl.ds(a, step)
        pltpu.make_async_copy(
            total.at[piece, :], out0.at[piece, :], semaphores.at[a // step]
        ).wait()


VMEM = pl.BlockSpec(memory_space=pltpu.VMEM)
HBM = pl.BlockSpec(memory_space=pl.ANY)


def call(kernel, operands, specs, out_shape, out_specs, scratch, pairs, aliases=None):
    width = operands[1].shape[1]
    return pl.pallas_call(
        kernel,
        in_specs=specs,
        out_specs=out_specs,
        out_shape=out_shape,
        scratch_shapes=scratch,
        input_output_aliases=aliases or {},
        cost_estimate=pl.CostEstimate(
            flops=4 * pairs * width, bytes_accessed=1 << 20, transcendentals=2 * pairs
        ),
        compiler_params=pltpu.CompilerParams(vmem_limit_bytes=20 * 1024 * 1024),
    )(*operands)


def shards(visual, caption, sharpness_scale, score_shift):
    blocks = lax.axis_size("blk")
    cells = blocks // 2
    even = lax.axis_index("blk") % 2 == 0
    rows, width = visual.shape

    def at(cell, half):
        return 2 * (cell % cells) + half

    cross = [(b, b ^ 1) for b in range(blocks)]
    outward = [(at(c, h), at(c + 1 - 2 * h, h)) for c in range(cells) for h in (0, 1)]
    inward = [(at(c, h), at(c - 1 + 2 * h, h)) for c in range(cells) for h in (0, 1)]

    def one(a, b):
        return jnp.where(even, caption[a:b], visual[a:b])

    def two(a, b):
        return jnp.where(even, visual[a:b], caption[a:b])

    def spans(sizes):
        ends = [sum(sizes[:k]) for k in range(len(sizes) + 1)]
        return list(zip(ends, ends[1:]))

    heads = one(0, FIRST[0]), two(0, SECOND[0])
    caption, visual = lax.optimization_barrier((caption, visual, heads))[:2]
    own1, own2 = one(0, rows), two(0, rows)
    flag = jnp.where(even, 0.0, 1.0)
    row = lax.broadcasted_iota(jnp.int32, (8, 128), 0)
    scalars = jnp.where(row == 0, sharpness_scale[0], jnp.where(row == 1, score_shift[0], flag))

    real = jax.ShapeDtypeStruct((rows, width), jnp.float32)
    half = jax.ShapeDtypeStruct((rows, width), jnp.bfloat16)

    def count(partners):
        return sum(p.shape[0] for p in partners)

    def units_of(partners):
        return pltpu.VMEM((max(count(partners), 16), width), jnp.bfloat16)

    def middle(unit, sums, partners):
        operands = [scalars, unit, sums, *partners]
        return call(
            functools.partial(middle_kernel, len(partners)),
            operands,
            [VMEM] + [VMEM] * (len(operands) - 1),
            real,
            VMEM,
            [units_of(partners)],
            rows * count(partners),
            {2: 0},
        )

    def last(side, own, unit, sums, partners, outs):
        operands = [scalars, own, unit, sums, *partners, *outs]
        n = len(operands)
        return call(
            functools.partial(last_kernel, len(partners), side),
            operands,
            [VMEM] + [VMEM] * (n - 1 - len(outs)) + [HBM] * len(outs),
            (real, real),
            (HBM, HBM),
            [units_of(partners), *staging],
            rows * count(partners),
            {n - 2: 0, n - 1: 1} if outs else {},
        )

    staging = [
        pltpu.VMEM((rows, width), jnp.float32),
        pltpu.SemaphoreType.DMA((rows // 128,)),
    ]

    there, ready = {}, {}
    for k, (a, b) in enumerate(spans(FIRST)):
        ready["r1", k] = functools.partial(one, a, b)
        ready["q1", k] = functools.partial(there.get, ("r1", k))
    for k, (a, b) in enumerate(spans(SECOND)):
        ready["s2", k] = functools.partial(two, a, b)
        ready["r2", k] = functools.partial(there.get, ("s2", k))
        ready["q2", k] = functools.partial(there.get, ("r2", k))
    ready["r1", 0], ready["s2", 0] = lambda: heads[0], lambda: heads[1]
    ready["s1", 0] = lambda: own1
    routes = {"r1": cross, "q1": inward, "s1": outward, "s2": inward, "r2": cross, "q2": outward}

    done, outs = (), ()
    sums, units = {}, {}
    for action, *names in PLAN:
        names = [(n[:2], int(n[2:] or 0)) for n in names]
        if action == "wait":
            done = tuple(there[n] if n in there else sums[int(n[0][1])] for n in names)
        elif action == "go":
            values = tuple(ready[n]() for n in names)
            if done:
                values = lax.optimization_barrier((values, done))[0]
            for n, value in zip(names, values):
                there[n] = lax.ppermute(value, "blk", routes[n[0]])
        elif action == "first":
            units[1], units[2], sums[1], sums[2] = call(
                first_kernel,
                [scalars, own1, own2],
                [VMEM, VMEM, VMEM],
                (half, half, real, real),
                (VMEM,) * 4,
                [pltpu.VMEM((rows, rows), jnp.bfloat16)],
                2 * rows * rows,
            )
        else:
            side = int(action[-1])
            partners = [there[n] for n in names]
            if action[:-1] == "add":
                sums[side] = middle(units[side], sums[side], partners)
            else:
                outs = last(side, (own1, own2)[side - 1], units[side], sums[side], partners, outs)
    return outs


def solution(mesh):
    placed = (P(("dp", "blk"), None), P(("dp", "blk"), None), P(), P())
    return jax.shard_map(
        shards,
        mesh=mesh,
        in_specs=placed,
        out_specs=(P(("dp", "blk"), None), P(("dp", "blk"), None)),
        check_vma=False,
    )
```
